32 devices in a mesh: row: 8 (over z, x), col: 4 (over y, core).
Axes of the slice: x: 2, y: 2, z: 4, core: 2. Of those that a mesh axis runs over, the one named last changes fastest.
Arguments:
- reflection: bfloat16 [2, 8, 6144, 6144], P(None, None, 'row', 'col'), may hold values from -0.0390625 to 0.0390625
- initial: bfloat16 [96, 2, 8, 6144], P('row', None, None, 'col'), may hold values from -6 to 6
- onset_down: int32 [96, 6144], P('col', 'row'), may hold values from 4 to 27
- onset_up: int32 [96, 6144], P('row', 'col'), may hold values from 4 to 27
Outputs:
- minus_field: float32 [96, 2, 8, 6144], P('col', None, None, 'row')
- plus_field: float32 [96, 2, 8, 6144], P('row', None, None, 'col')
The draws below stay inside these ranges and needn't reach their ends.
All inputs are finite; a program needn't handle non-finite values.
Results may differ from the reference program's by a relative error of at most 0.019.
Values may be sent and summed in bfloat16 or wider, within the bound.
A program may use at most 128 MiB of HBM per device.

```python
import math
import jax
import jax.numpy as jnp
from jax import lax

NS = 6144
NF = 8
NT = 32
NV = 96
ITERS = 2
N_ROW = 8
N_COL = 4


def touch_ends(drawn, key, smallest, largest):
    spot = [jax.random.randint(jax.random.fold_in(key, axis), (), 0, length) for axis, length in enumerate(drawn.shape)]
    longest = drawn.shape.index(max(drawn.shape))
    beside = spot[:longest] + [(spot[longest] + 1) % drawn.shape[longest]] + spot[longest + 1:]
    return drawn.at[tuple(spot)].set(smallest).at[tuple(beside)].set(largest)


def levels(key, extent, split, smallest, top_value):
    level = 1.0
    for axis_at, blocks in split:
        steps = jax.random.uniform(jax.random.fold_in(jax.random.fold_in(key, 6), axis_at), (blocks,), jnp.float32, smallest / len(split), top_value / len(split))
        level = level * jnp.repeat(jnp.exp(steps), extent[axis_at] // blocks).reshape((-1,) + (1,) * (len(extent) - 1 - axis_at))
    return level


def scatter_about(own_key, shape, spread, reach, cuts=(), held_as=jnp.bfloat16):
    values = jax.random.normal(own_key, shape, jnp.float32) * spread
    if len(cuts) > 0:
        values = levels(own_key, shape, cuts, -0.22, 0.18) * values
    return jnp.clip(values, min=-reach, max=reach).astype(held_as)


def setup_inputs(seed: int = 0) -> dict:
    key_of = jax.random.split(jax.random.key(seed), 5)
    reflection = scatter_about(key_of[0], (2, NF, NS, NS), (4 * NS) ** -0.5, 0.0390625, ((2, 8), (3, 4)))
    initial = scatter_about(key_of[1], (NV, 2, NF, NS), 1.0, 6.0, ((0, 8), (3, 4)))
    onset_down = touch_ends(jax.random.randint(key_of[2], (NV, NS), 4, NT - 4), jax.random.fold_in(key_of[2], 1), 4, (NT - 4) - 1).astype(jnp.int32)
    onset_up = touch_ends(jax.random.randint(key_of[3], (NV, NS), 4, NT - 4), jax.random.fold_in(key_of[3], 1), 4, (NT - 4) - 1).astype(jnp.int32)
    return {"reflection": reflection, "initial": initial, "onset_down": onset_down, "onset_up": onset_up}


def dft_tables(freq_count, time_count):
    time_index = lax.broadcasted_iota(jnp.int32, (time_count, freq_count), 0)
    orders = lax.broadcasted_iota(jnp.int32, (time_count, freq_count), 1) + 2
    phases = (time_index * orders) % time_count
    angles = phases.astype(jnp.float32) * (2.0 * math.pi / time_count)
    to_time = jnp.concatenate([jnp.cos(angles), -jnp.sin(angles)], axis=1)
    to_freq = to_time.T * (2.0 / time_count)
    return to_time, to_freq


def window(spectra, onsets):
    to_time, to_freq = dft_tables(spectra.shape[2], NT)
    flattened = spectra.reshape(spectra.shape[0], 2 * spectra.shape[2], spectra.shape[3])
    series = jnp.einsum("tq,vqs->vts", to_time, flattened, precision=lax.Precision.HIGHEST)
    moments = lax.broadcasted_iota(jnp.int32, (1, NT, 1), 1)
    keep_mask = moments < onsets[:, None, :]
    series = jnp.where(keep_mask, series, jnp.zeros_like(series))
    spectrum = jnp.einsum("qt,vts->vqs", to_freq, series, precision=lax.Precision.HIGHEST)
    return spectrum.reshape(spectra.shape)


def forward(reflection, plus_low):
    blocks = NS // N_COL

    def add_block(totals, block_index):
        first_col = block_index * blocks
        refl_slab = lax.dynamic_slice_in_dim(reflection, first_col, blocks, 3).astype(jnp.float32)
        focus = lax.dynamic_slice_in_dim(plus_low, first_col, blocks, 3).astype(jnp.float32)
        prec = lax.Precision.HIGHEST
        real_part = jnp.einsum("nsk,vnk->vns", refl_slab[0], focus[:, 0], precision=prec) - jnp.einsum("nsk,vnk->vns", refl_slab[1], focus[:, 1], precision=prec)
        imag_part = jnp.einsum("nsk,vnk->vns", refl_slab[0], focus[:, 1], precision=prec) + jnp.einsum("nsk,vnk->vns", refl_slab[1], focus[:, 0], precision=prec)
        rounded = lax.optimization_barrier(jnp.stack([real_part, imag_part], axis=1).astype(jnp.bfloat16))
        return totals + rounded.astype(jnp.float32), None

    start_value = jnp.zeros((plus_low.shape[0], 2, NF, NS), jnp.float32)
    totals, leftover = lax.scan(add_block, start_value, jnp.arange(N_COL, dtype=jnp.int32))
    return totals


def adjoint(reflection, minus_low):
    blocks = NS // N_ROW

    def add_block(totals, block_index):
        first_row = block_index * blocks
        refl_slab = lax.dynamic_slice_in_dim(reflection, first_row, blocks, 2).astype(jnp.float32)
        moving = lax.dynamic_slice_in_dim(minus_low, first_row, blocks, 3).astype(jnp.float32)
        prec = lax.Precision.HIGHEST
        real_part = jnp.einsum("nsk,vns->vnk", refl_slab[0], moving[:, 0], precision=prec) + jnp.einsum("nsk,vns->vnk", refl_slab[1], moving[:, 1], precision=prec)
        imag_part = jnp.einsum("nsk,vns->vnk", refl_slab[0], moving[:, 1], precision=prec) - jnp.einsum("nsk,vns->vnk", refl_slab[1], moving[:, 0], precision=prec)
        rounded = lax.optimization_barrier(jnp.stack([real_part, imag_part], axis=1).astype(jnp.bfloat16))
        return totals + rounded.astype(jnp.float32), None

    start_value = jnp.zeros((minus_low.shape[0], 2, NF, NS), jnp.float32)
    totals, leftover = lax.scan(add_block, start_value, jnp.arange(N_ROW, dtype=jnp.int32))
    return totals


def reference(reflection, initial, onset_down, onset_up):
    plus_low = initial
    minus_field = jnp.zeros(initial.shape, jnp.float32)
    plus_field = initial.astype(jnp.float32)
    for iteration in range(ITERS):
        minus_field = window(forward(reflection, plus_low), onset_down)
        minus_low = minus_field.astype(jnp.bfloat16)
        plus_field = initial.astype(jnp.float32) + window(adjoint(reflection, minus_low), onset_up)
        plus_low = plus_field.astype(jnp.bfloat16)
    return minus_field, plus_field
```

```python
import functools
import math

import jax
import jax.numpy as jnp
from jax import lax
from jax.experimental import pallas as pl
from jax.experimental.pallas import tpu as pltpu
from jax.sharding import PartitionSpec as P

NT = 32
ITERS = 2
MESH = pl.DeviceIdType.MESH


def dft_tables(freq_count, time_count):
    time_index = lax.broadcasted_iota(jnp.int32, (time_count, freq_count), 0)
    orders = lax.broadcasted_iota(jnp.int32, (time_count, freq_count), 1) + 2
    phases = time_index * orders % time_count
    angles = phases.astype(jnp.float32) * (2.0 * math.pi / time_count)
    to_time = jnp.concatenate([jnp.cos(angles), -jnp.sin(angles)], axis=1)
    to_freq = to_time.T * (2.0 / time_count)
    return (to_time, to_freq)


def window(flattened, onsets):
    to_time, to_freq = dft_tables(flattened.shape[1] // 2, NT)
    series = jnp.einsum("tq,vqs->vts", to_time, flattened, precision=lax.Precision.HIGHEST)
    moments = lax.broadcasted_iota(jnp.int32, (1, NT, 1), 1)
    keep_mask = moments < onsets[:, None, :]
    series = jnp.where(keep_mask, series, jnp.zeros_like(series))
    return jnp.einsum("qt,vts->vqs", to_freq, series, precision=lax.Precision.HIGHEST)


def place_of(row, count):
    z, x = row // 2, row % 2
    return z + x * (count - 1 - 2 * z)


def row_of(place, count):
    half = place // (count // 2)
    return (1 - half) * 2 * place + half * (2 * (count - 1 - place) + 1)


def greet(right, left):
    barrier = pltpu.get_barrier_semaphore()
    for neighbour in (left, right):
        pl.semaphore_signal(barrier, inc=1, device_id={"row": neighbour}, device_id_type=MESH)
    pl.semaphore_wait(barrier, 2)


def chunks_of(length):
    count = 4 if length % 4 == 0 else 1
    return count, length // count


def goes(way, distance, chunk, chunks, count):
    if distance < count // 2:
        return True
    return (chunk < (chunks + 1) // 2) == (way == 0)


def gather_kernel(count, block_ref, out_ref, own_sem, send_sem, recv_sem):
    place = place_of(lax.axis_index("row"), count)
    neighbours = [row_of((place + 1) % count, count), row_of((place + count - 1) % count, count)]
    length = block_ref.shape[0]
    chunks, size = chunks_of(length)
    greet(neighbours[0], neighbours[1])
    me = lax.axis_index("row")
    own = pltpu.make_async_copy(block_ref, out_ref.at[pl.ds(me * length, length)], own_sem)
    own.start()

    started = {}
    for distance in range(1, count // 2 + 1):
        for chunk in range(chunks):
            for way in (0, 1):
                if distance > 1 and (way, distance - 1, chunk) in started:
                    started[(way, distance - 1, chunk)].wait_recv()
                if not goes(way, distance, chunk, chunks, count):
                    continue
                back = count - distance + 1 if way == 0 else distance - 1
                owner = row_of((place + back) % count, count)
                spot = pl.ds(owner * length + chunk * size, size)
                source = block_ref.at[pl.ds(chunk * size, size)] if distance == 1 else out_ref.at[spot]
                copy = pltpu.make_async_remote_copy(
                    src_ref=source,
                    dst_ref=out_ref.at[spot],
                    send_sem=send_sem.at[way, distance - 1, chunk],
                    recv_sem=recv_sem.at[way, distance - 1, chunk],
                    device_id={"row": neighbours[way]},
                    device_id_type=MESH,
                )
                copy.start()
                started[(way, distance, chunk)] = copy
    for (way, distance, chunk), copy in started.items():
        if distance == count // 2:
            copy.wait_recv()
    for copy in started.values():
        copy.wait_send()
    own.wait()


def gather_row(block, count):
    chunks, _ = chunks_of(block.shape[0])
    shape = (count * block.shape[0],) + block.shape[1:]
    return pl.pallas_call(
        functools.partial(gather_kernel, count),
        out_shape=jax.ShapeDtypeStruct(shape, block.dtype),
        in_specs=[pl.BlockSpec(memory_space=pltpu.VMEM)],
        out_specs=pl.BlockSpec(memory_space=pltpu.VMEM),
        scratch_shapes=[
            pltpu.SemaphoreType.DMA,
            pltpu.SemaphoreType.DMA((2, count // 2, chunks)),
            pltpu.SemaphoreType.DMA((2, count // 2, chunks)),
        ],
        compiler_params=pltpu.CompilerParams(
            collective_id=0, has_side_effects=True, vmem_limit_bytes=32 * 1024 * 1024
        ),
        cost_estimate=pl.CostEstimate(flops=0, bytes_accessed=16 * block.size, transcendentals=0),
    )(block)


def scatter_kernel(count, terms_ref, out_ref, held, send_sem, recv_sem):
    place = place_of(lax.axis_index("row"), count)
    neighbours = [row_of((place + 1) % count, count), row_of((place + count - 1) % count, count)]
    length = out_ref.shape[0]
    chunks, size = chunks_of(length)
    greet(neighbours[0], neighbours[1])
    me = lax.axis_index("row")

    started = {}
    for distance in range(count // 2, 0, -1):
        for chunk in range(chunks):
            for way in (0, 1):
                if not goes(way, distance, chunk, chunks, count):
                    continue
                ahead = distance if way == 0 else count - distance
                target = row_of((place + ahead) % count, count)
                term = terms_ref.at[pl.ds(target * length + chunk * size, size)]
                part = pl.ds(chunk * size, size)
                if (way, distance + 1, chunk) in started:
                    started[(way, distance + 1, chunk)].wait_recv()
                    source = held.at[way, distance, part]
                    source[...] = (source[...].astype(jnp.float32) + term[...].astype(jnp.float32)).astype(
                        source.dtype
                    )
                else:
                    source = term
                copy = pltpu.make_async_remote_copy(
                    src_ref=source,
                    dst_ref=held.at[way, distance - 1, part],
                    send_sem=send_sem.at[way, distance - 1, chunk],
                    recv_sem=recv_sem.at[way, distance - 1, chunk],
                    device_id={"row": neighbours[way]},
                    device_id_type=MESH,
                )
                copy.start()
                started[(way, distance, chunk)] = copy
    for chunk in range(chunks):
        part = pl.ds(chunk * size, size)
        total = terms_ref[pl.ds(me * length + chunk * size, size)].astype(jnp.float32)
        for way in (0, 1):
            started[(way, 1, chunk)].wait_recv()
            total += held[way, 0, part].astype(jnp.float32)
        out_ref[part] = total
    for copy in started.values():
        copy.wait_send()


def scatter_row(terms, count):
    length = terms.shape[0] // count
    chunks, _ = chunks_of(length)
    tail = terms.shape[1:]
    return pl.pallas_call(
        functools.partial(scatter_kernel, count),
        out_shape=jax.ShapeDtypeStruct((length,) + tail, jnp.float32),
        in_specs=[pl.BlockSpec(memory_space=pltpu.VMEM)],
        out_specs=pl.BlockSpec(memory_space=pltpu.VMEM),
        scratch_shapes=[
            pltpu.VMEM((2, count // 2, length) + tail, terms.dtype),
            pltpu.SemaphoreType.DMA((2, count // 2, chunks)),
            pltpu.SemaphoreType.DMA((2, count // 2, chunks)),
        ],
        compiler_params=pltpu.CompilerParams(
            collective_id=1, has_side_effects=True, vmem_limit_bytes=32 * 1024 * 1024
        ),
        cost_estimate=pl.CostEstimate(flops=0, bytes_accessed=4 * terms.size, transcendentals=0),
    )(terms)


def forward_local(reflection, focus):
    freqs = reflection.shape[1]
    parts = focus.reshape(focus.shape[0], 2, freqs, focus.shape[2])
    by_real = jnp.einsum("nsk,vonk->novs", reflection[0], parts, preferred_element_type=jnp.float32)
    by_imag = jnp.einsum("nsk,vonk->novs", reflection[1], parts, preferred_element_type=jnp.float32)
    real_part = by_real[:, 0] - by_imag[:, 1]
    imag_part = by_real[:, 1] + by_imag[:, 0]
    both = jnp.stack([real_part, imag_part], axis=0).astype(jnp.bfloat16)
    return both.reshape((2 * freqs,) + both.shape[2:]).transpose(1, 0, 2)


def adjoint_local(reflection, moving):
    freqs = reflection.shape[1]
    parts = moving.reshape(moving.shape[0], 2, freqs, moving.shape[2])
    by_real = jnp.einsum("nsk,vons->novk", reflection[0], parts, preferred_element_type=jnp.float32)
    by_imag = jnp.einsum("nsk,vons->novk", reflection[1], parts, preferred_element_type=jnp.float32)
    real_part = by_real[:, 0] + by_imag[:, 1]
    imag_part = by_real[:, 1] - by_imag[:, 0]
    both = jnp.stack([real_part, imag_part], axis=0).astype(jnp.bfloat16)
    return both.reshape((2 * freqs,) + both.shape[2:]).transpose(1, 0, 2)


def body(rows, reflection, initial, onset_down, onset_up):
    freqs = initial.shape[2]
    own = initial.reshape(initial.shape[0], 2 * freqs, initial.shape[3])
    focus_low = own
    minus_field = None
    plus_field = None
    for iteration in range(ITERS):
        focus = gather_row(focus_low, rows)
        summed = lax.psum_scatter(
            forward_local(reflection, focus), "col", scatter_dimension=0, tiled=True
        ).astype(jnp.float32)
        minus_field = window(summed, onset_down)
        moving_all = lax.all_gather(minus_field.astype(jnp.bfloat16), "col", axis=0, tiled=True)
        summed_up = scatter_row(adjoint_local(reflection, moving_all), rows)
        plus_field = own.astype(jnp.float32) + window(summed_up, onset_up)
        focus_low = plus_field.astype(jnp.bfloat16)
    return tuple(
        field.reshape(field.shape[0], 2, freqs, field.shape[2]) for field in (minus_field, plus_field)
    )


def solution(mesh):
    return jax.shard_map(
        functools.partial(body, mesh.shape["row"]),
        mesh=mesh,
        in_specs=(
            P(None, None, "row", "col"),
            P("row", None, None, "col"),
            P("col", "row"),
            P("row", "col"),
        ),
        out_specs=(P("col", None, None, "row"), P("row", None, None, "col")),
        check_vma=False,
    )
```

```python
import functools
import math

import jax
import jax.numpy as jnp
from jax import lax
from jax.experimental import pallas as pl
from jax.experimental.pallas import tpu as pltpu
from jax.sharding import PartitionSpec as P

NT = 32
ITERS = 2
MESH = pl.DeviceIdType.MESH


def dft_tables(freq_count, time_count):
    time_index = lax.broadcasted_iota(jnp.int32, (time_count, freq_count), 0)
    orders = lax.broadcasted_iota(jnp.int32, (time_count, freq_count), 1) + 2
    phases = time_index * orders % time_count
    angles = phases.astype(jnp.float32) * (2.0 * math.pi / time_count)
    to_time = jnp.concatenate([jnp.cos(angles), -jnp.sin(angles)], axis=1)
    to_freq = to_time.T * (2.0 / time_count)
    return (to_time, to_freq)


def window(flattened, onsets):
    to_time, to_freq = dft_tables(flattened.shape[1] // 2, NT)
    series = jnp.einsum("tq,vqs->vts", to_time, flattened, precision=lax.Precision.HIGHEST)
    moments = lax.broadcasted_iota(jnp.int32, (1, NT, 1), 1)
    keep_mask = moments < onsets[:, None, :]
    series = jnp.where(keep_mask, series, jnp.zeros_like(series))
    return jnp.einsum("qt,vts->vqs", to_freq, series, precision=lax.Precision.HIGHEST)


def place_of(row, count):
    z, x = row // 2, row % 2
    return z + x * (count - 1 - 2 * z)


def row_of(place, count):
    half = place // (count // 2)
    return (1 - half) * 2 * place + half * (2 * (count - 1 - place) + 1)


def greet(axis, right, left):
    barrier = pltpu.get_barrier_semaphore()
    for neighbour in (left, right):
        pl.semaphore_signal(barrier, inc=1, device_id={axis: neighbour}, device_id_type=MESH)
    pl.semaphore_wait(barrier, 2)


def chunks_of(length):
    count = 4 if length % 4 == 0 else 1
    return count, length // count


def goes(way, distance, chunk, chunks, count):
    if distance < count // 2:
        return True
    return (chunk < (chunks + 1) // 2) == (way == 0)


def gather_kernel(axis, count, block_ref, out_ref, own_sem, send_sem, recv_sem):
    place = place_of(lax.axis_index(axis), count)
    neighbours = [row_of((place + 1) % count, count), row_of((place + count - 1) % count, count)]
    length = block_ref.shape[0]
    chunks, size = chunks_of(length)
    greet(axis, neighbours[0], neighbours[1])
    me = lax.axis_index(axis)
    own = pltpu.make_async_copy(block_ref, out_ref.at[pl.ds(me * length, length)], own_sem)
    own.start()

    started = {}
    for distance in range(1, count // 2 + 1):
        for chunk in range(chunks):
            for way in (0, 1):
                if distance > 1 and (way, distance - 1, chunk) in started:
                    started[(way, distance - 1, chunk)].wait_recv()
                if not goes(way, distance, chunk, chunks, count):
                    continue
                back = count - distance + 1 if way == 0 else distance - 1
                owner = row_of((place + back) % count, count)
                spot = pl.ds(owner * length + chunk * size, size)
                source = block_ref.at[pl.ds(chunk * size, size)] if distance == 1 else out_ref.at[spot]
                copy = pltpu.make_async_remote_copy(
                    src_ref=source,
                    dst_ref=out_ref.at[spot],
                    send_sem=send_sem.at[way, distance - 1, chunk],
                    recv_sem=recv_sem.at[way, distance - 1, chunk],
                    device_id={axis: neighbours[way]},
                    device_id_type=MESH,
                )
                copy.start()
                started[(way, distance, chunk)] = copy
    for (way, distance, chunk), copy in started.items():
        if distance == count // 2:
            copy.wait_recv()
    for copy in started.values():
        copy.wait_send()
    own.wait()


def gather_ring(block, axis, count, number):
    chunks, _ = chunks_of(block.shape[0])
    shape = (count * block.shape[0],) + block.shape[1:]
    return pl.pallas_call(
        functools.partial(gather_kernel, axis, count),
        out_shape=jax.ShapeDtypeStruct(shape, block.dtype),
        in_specs=[pl.BlockSpec(memory_space=pltpu.VMEM)],
        out_specs=pl.BlockSpec(memory_space=pltpu.VMEM),
        scratch_shapes=[
            pltpu.SemaphoreType.DMA,
            pltpu.SemaphoreType.DMA((2, count // 2, chunks)),
            pltpu.SemaphoreType.DMA((2, count // 2, chunks)),
        ],
        compiler_params=pltpu.CompilerParams(
            collective_id=number, has_side_effects=True, vmem_limit_bytes=32 * 1024 * 1024
        ),
        cost_estimate=pl.CostEstimate(flops=0, bytes_accessed=16 * block.size, transcendentals=0),
    )(block)


def scatter_kernel(axis, count, terms_ref, out_ref, held, send_sem, recv_sem):
    place = place_of(lax.axis_index(axis), count)
    neighbours = [row_of((place + 1) % count, count), row_of((place + count - 1) % count, count)]
    length = out_ref.shape[0]
    chunks, size = chunks_of(length)
    greet(axis, neighbours[0], neighbours[1])
    me = lax.axis_index(axis)

    started = {}
    for distance in range(count // 2, 0, -1):
        for chunk in range(chunks):
            for way in (0, 1):
                if not goes(way, distance, chunk, chunks, count):
                    continue
                ahead = distance if way == 0 else count - distance
                target = row_of((place + ahead) % count, count)
                term = terms_ref.at[pl.ds(target * length + chunk * size, size)]
                part = pl.ds(chunk * size, size)
                if (way, distance + 1, chunk) in started:
                    started[(way, distance + 1, chunk)].wait_recv()
                    source = held.at[way, distance, part]
                    source[...] = (source[...].astype(jnp.float32) + term[...].astype(jnp.float32)).astype(
                        source.dtype
                    )
                else:
                    source = term
                copy = pltpu.make_async_remote_copy(
                    src_ref=source,
                    dst_ref=held.at[way, distance - 1, part],
                    send_sem=send_sem.at[way, distance - 1, chunk],
                    recv_sem=recv_sem.at[way, distance - 1, chunk],
                    device_id={axis: neighbours[way]},
                    device_id_type=MESH,
                )
                copy.start()
                started[(way, distance, chunk)] = copy
    for chunk in range(chunks):
        part = pl.ds(chunk * size, size)
        total = terms_ref[pl.ds(me * length + chunk * size, size)].astype(jnp.float32)
        for way in (0, 1):
            started[(way, 1, chunk)].wait_recv()
            total += held[way, 0, part].astype(jnp.float32)
        out_ref[part] = total
    for copy in started.values():
        copy.wait_send()


def scatter_ring(terms, axis, count, number):
    length = terms.shape[0] // count
    chunks, _ = chunks_of(length)
    tail = terms.shape[1:]
    return pl.pallas_call(
        functools.partial(scatter_kernel, axis, count),
        out_shape=jax.ShapeDtypeStruct((length,) + tail, jnp.float32),
        in_specs=[pl.BlockSpec(memory_space=pltpu.VMEM)],
        out_specs=pl.BlockSpec(memory_space=pltpu.VMEM),
        scratch_shapes=[
            pltpu.VMEM((2, count // 2, length) + tail, terms.dtype),
            pltpu.SemaphoreType.DMA((2, count // 2, chunks)),
            pltpu.SemaphoreType.DMA((2, count // 2, chunks)),
        ],
        compiler_params=pltpu.CompilerParams(
            collective_id=number, has_side_effects=True, vmem_limit_bytes=32 * 1024 * 1024
        ),
        cost_estimate=pl.CostEstimate(flops=0, bytes_accessed=4 * terms.size, transcendentals=0),
    )(terms)


def product_kernel(contract, sign, refl_ref, field_ref, out_ref):
    dims = (((1,), (contract,)), ((), ()))
    field = field_ref[0]
    by_real = lax.dot_general(field, refl_ref[0, 0], dims, preferred_element_type=jnp.float32)
    by_imag = lax.dot_general(field, refl_ref[1, 0], dims, preferred_element_type=jnp.float32)
    half = field.shape[0] // 2
    out_ref[0, 0] = (by_real[:half] - sign * by_imag[half:]).astype(out_ref.dtype)
    out_ref[0, 1] = (by_real[half:] + sign * by_imag[:half]).astype(out_ref.dtype)


def product_local(reflection, field, contract, sign):
    _, freqs, s_count, k_count = reflection.shape
    count, _, inside = field.shape
    outside = s_count if contract == 1 else k_count
    by_freq = field.reshape(count, 2, freqs, inside).transpose(2, 1, 0, 3).reshape(freqs, 2 * count, inside)
    terms = pl.pallas_call(
        functools.partial(product_kernel, contract, sign),
        grid=(freqs,),
        out_shape=jax.ShapeDtypeStruct((freqs, 2, count, outside), jnp.bfloat16),
        in_specs=[
            pl.BlockSpec((2, 1, s_count, k_count), lambda n: (0, n, 0, 0)),
            pl.BlockSpec((1, 2 * count, inside), lambda n: (n, 0, 0)),
        ],
        out_specs=pl.BlockSpec((1, 2, count, outside), lambda n: (n, 0, 0, 0)),
        compiler_params=pltpu.CompilerParams(vmem_limit_bytes=40 * 1024 * 1024),
    )(reflection, by_freq)
    return terms.transpose(2, 1, 0, 3).reshape(count, 2 * freqs, outside)


def body(rows, cols, reflection, initial, onset_down, onset_up):
    freqs = initial.shape[2]
    own = initial.reshape(initial.shape[0], 2 * freqs, initial.shape[3])
    focus_low = own
    minus_field = None
    plus_field = None
    for iteration in range(ITERS):
        focus = gather_ring(focus_low, "row", rows, 0)
        summed = scatter_ring(product_local(reflection, focus, 1, 1.0), "col", cols, 2)
        minus_field = window(summed, onset_down)
        moving_all = gather_ring(minus_field.astype(jnp.bfloat16), "col", cols, 3)
        summed_up = scatter_ring(product_local(reflection, moving_all, 0, -1.0), "row", rows, 1)
        plus_field = own.astype(jnp.float32) + window(summed_up, onset_up)
        focus_low = plus_field.astype(jnp.bfloat16)
    return tuple(
        field.reshape(field.shape[0], 2, freqs, field.shape[2]) for field in (minus_field, plus_field)
    )


def solution(mesh):
    return jax.shard_map(
        functools.partial(body, mesh.shape["row"], mesh.shape["col"]),
        mesh=mesh,
        in_specs=(
            P(None, None, "row", "col"),
            P("row", None, None, "col"),
            P("col", "row"),
            P("row", "col"),
        ),
        out_specs=(P("col", None, None, "row"), P("row", None, None, "col")),
        check_vma=False,
    )
```

```python
import functools
import math

import jax
import jax.numpy as jnp
from jax import lax
from jax.experimental import pallas as pl
from jax.experimental.pallas import tpu as pltpu
from jax.sharding import PartitionSpec as P

NT = 32
ITERS = 2
MESH = pl.DeviceIdType.MESH


def dft_tables(freq_count, time_count):
    time_index = lax.broadcasted_iota(jnp.int32, (time_count, freq_count), 0)
    orders = lax.broadcasted_iota(jnp.int32, (time_count, freq_count), 1) + 2
    phases = time_index * orders % time_count
    angles = phases.astype(jnp.float32) * (2.0 * math.pi / time_count)
    to_time = jnp.concatenate([jnp.cos(angles), -jnp.sin(angles)], axis=1)
    to_freq = to_time.T * (2.0 / time_count)
    return (to_time, to_freq)


def window(flattened, onsets):
    to_time, to_freq = dft_tables(flattened.shape[1] // 2, NT)
    series = jnp.einsum("tq,vqs->vts", to_time, flattened, precision=lax.Precision.HIGHEST)
    moments = lax.broadcasted_iota(jnp.int32, (1, NT, 1), 1)
    keep_mask = moments < onsets[:, None, :]
    series = jnp.where(keep_mask, series, jnp.zeros_like(series))
    return jnp.einsum("qt,vts->vqs", to_freq, series, precision=lax.Precision.HIGHEST)


def place_of(row, count):
    z, x = row // 2, row % 2
    return z + x * (count - 1 - 2 * z)


def row_of(place, count):
    half = place // (count // 2)
    return (1 - half) * 2 * place + half * (2 * (count - 1 - place) + 1)


def greet(axis, right, left):
    barrier = pltpu.get_barrier_semaphore()
    for neighbour in (left, right):
        pl.semaphore_signal(barrier, inc=1, device_id={axis: neighbour}, device_id_type=MESH)
    pl.semaphore_wait(barrier, 2)


def chunks_of(length):
    count = 6 if length % 6 == 0 else 1
    return count, length // count


def goes(way, distance, chunk, chunks, count):
    if distance < count // 2:
        return True
    return (chunk < (chunks + 1) // 2) == (way == 0)


def gather_kernel(axis, count, block_ref, out_ref, own_sem, send_sem, recv_sem):
    place = place_of(lax.axis_index(axis), count)
    neighbours = [row_of((place + 1) % count, count), row_of((place + count - 1) % count, count)]
    length = block_ref.shape[0]
    chunks, size = chunks_of(length)
    greet(axis, neighbours[0], neighbours[1])
    me = lax.axis_index(axis)
    own = pltpu.make_async_copy(block_ref, out_ref.at[pl.ds(me * length, length)], own_sem)
    own.start()

    started = {}
    for distance in range(1, count // 2 + 1):
        for chunk in range(chunks):
            for way in (0, 1):
                if distance > 1 and (way, distance - 1, chunk) in started:
                    started[(way, distance - 1, chunk)].wait_recv()
                if not goes(way, distance, chunk, chunks, count):
                    continue
                back = count - distance + 1 if way == 0 else distance - 1
                owner = row_of((place + back) % count, count)
                spot = pl.ds(owner * length + chunk * size, size)
                source = block_ref.at[pl.ds(chunk * size, size)] if distance == 1 else out_ref.at[spot]
                copy = pltpu.make_async_remote_copy(
                    src_ref=source,
                    dst_ref=out_ref.at[spot],
                    send_sem=send_sem.at[way, distance - 1, chunk],
                    recv_sem=recv_sem.at[way, distance - 1, chunk],
                    device_id={axis: neighbours[way]},
                    device_id_type=MESH,
                )
                copy.start()
                started[(way, distance, chunk)] = copy
    for (way, distance, chunk), copy in started.items():
        if distance == count // 2:
            copy.wait_recv()
    for copy in started.values():
        copy.wait_send()
    own.wait()


def gather_ring(block, axis, count, number):
    chunks, _ = chunks_of(block.shape[0])
    shape = (count * block.shape[0],) + block.shape[1:]
    return pl.pallas_call(
        functools.partial(gather_kernel, axis, count),
        out_shape=jax.ShapeDtypeStruct(shape, block.dtype),
        in_specs=[pl.BlockSpec(memory_space=pltpu.VMEM)],
        out_specs=pl.BlockSpec(memory_space=pltpu.VMEM),
        scratch_shapes=[
            pltpu.SemaphoreType.DMA,
            pltpu.SemaphoreType.DMA((2, count // 2, chunks)),
            pltpu.SemaphoreType.DMA((2, count // 2, chunks)),
        ],
        compiler_params=pltpu.CompilerParams(
            collective_id=number, has_side_effects=True, vmem_limit_bytes=32 * 1024 * 1024
        ),
        cost_estimate=pl.CostEstimate(flops=0, bytes_accessed=16 * block.size, transcendentals=0),
    )(block)


def scatter_kernel(axis, count, terms_ref, out_ref, held, send_sem, recv_sem):
    place = place_of(lax.axis_index(axis), count)
    neighbours = [row_of((place + 1) % count, count), row_of((place + count - 1) % count, count)]
    length = out_ref.shape[0]
    chunks, size = chunks_of(length)
    greet(axis, neighbours[0], neighbours[1])
    me = lax.axis_index(axis)

    started = {}
    for distance in range(count // 2, 0, -1):
        for chunk in range(chunks):
            for way in (0, 1):
                if not goes(way, distance, chunk, chunks, count):
                    continue
                ahead = distance if way == 0 else count - distance
                target = row_of((place + ahead) % count, count)
                term = terms_ref.at[pl.ds(target * length + chunk * size, size)]
                part = pl.ds(chunk * size, size)
                if (way, distance + 1, chunk) in started:
                    started[(way, distance + 1, chunk)].wait_recv()
                    source = held.at[way, distance, part]
                    source[...] = (source[...].astype(jnp.float32) + term[...].astype(jnp.float32)).astype(
                        source.dtype
                    )
                else:
                    source = term
                copy = pltpu.make_async_remote_copy(
                    src_ref=source,
                    dst_ref=held.at[way, distance - 1, part],
                    send_sem=send_sem.at[way, distance - 1, chunk],
                    recv_sem=recv_sem.at[way, distance - 1, chunk],
                    device_id={axis: neighbours[way]},
                    device_id_type=MESH,
                )
                copy.start()
                started[(way, distance, chunk)] = copy
    for chunk in range(chunks):
        part = pl.ds(chunk * size, size)
        total = terms_ref[pl.ds(me * length + chunk * size, size)].astype(jnp.float32)
        for way in (0, 1):
            started[(way, 1, chunk)].wait_recv()
            total += held[way, 0, part].astype(jnp.float32)
        out_ref[part] = total
    for copy in started.values():
        copy.wait_send()


def scatter_ring(terms, axis, count, number):
    length = terms.shape[0] // count
    chunks, _ = chunks_of(length)
    tail = terms.shape[1:]
    return pl.pallas_call(
        functools.partial(scatter_kernel, axis, count),
        out_shape=jax.ShapeDtypeStruct((length,) + tail, jnp.float32),
        in_specs=[pl.BlockSpec(memory_space=pltpu.VMEM)],
        out_specs=pl.BlockSpec(memory_space=pltpu.VMEM),
        scratch_shapes=[
            pltpu.VMEM((2, count // 2, length) + tail, terms.dtype),
            pltpu.SemaphoreType.DMA((2, count // 2, chunks)),
            pltpu.SemaphoreType.DMA((2, count // 2, chunks)),
        ],
        compiler_params=pltpu.CompilerParams(
            collective_id=number, has_side_effects=True, vmem_limit_bytes=32 * 1024 * 1024
        ),
        cost_estimate=pl.CostEstimate(flops=0, bytes_accessed=4 * terms.size, transcendentals=0),
    )(terms)


def product_kernel(contract, sign, refl_ref, field_ref, out_ref):
    dims = (((1,), (contract,)), ((), ()))
    field = field_ref[0]
    by_real = lax.dot_general(field, refl_ref[0, 0], dims, preferred_element_type=jnp.float32)
    by_imag = lax.dot_general(field, refl_ref[1, 0], dims, preferred_element_type=jnp.float32)
    half = field.shape[0] // 2
    out_ref[0, 0] = (by_real[:half] - sign * by_imag[half:]).astype(out_ref.dtype)
    out_ref[0, 1] = (by_real[half:] + sign * by_imag[:half]).astype(out_ref.dtype)


def product_local(reflection, field, contract, sign):
    _, freqs, s_count, k_count = reflection.shape
    count, _, inside = field.shape
    outside = s_count if contract == 1 else k_count
    by_freq = field.reshape(count, 2, freqs, inside).transpose(2, 1, 0, 3).reshape(freqs, 2 * count, inside)
    terms = pl.pallas_call(
        functools.partial(product_kernel, contract, sign),
        grid=(freqs,),
        out_shape=jax.ShapeDtypeStruct((freqs, 2, count, outside), jnp.bfloat16),
        in_specs=[
            pl.BlockSpec((2, 1, s_count, k_count), lambda n: (0, n, 0, 0)),
            pl.BlockSpec((1, 2 * count, inside), lambda n: (n, 0, 0)),
        ],
        out_specs=pl.BlockSpec((1, 2, count, outside), lambda n: (n, 0, 0, 0)),
        compiler_params=pltpu.CompilerParams(vmem_limit_bytes=40 * 1024 * 1024),
    )(reflection, by_freq)
    return terms.transpose(2, 1, 0, 3).reshape(count, 2 * freqs, outside)


def body(rows, cols, reflection, initial, onset_down, onset_up):
    freqs = initial.shape[2]
    own = initial.reshape(initial.shape[0], 2 * freqs, initial.shape[3])
    focus_low = own
    minus_field = None
    plus_field = None
    for iteration in range(ITERS):
        focus = gather_ring(focus_low, "row", rows, 0)
        summed = scatter_ring(product_local(reflection, focus, 1, 1.0), "col", cols, 2)
        minus_field = window(summed, onset_down)
        moving_all = gather_ring(minus_field.astype(jnp.bfloat16), "col", cols, 3)
        summed_up = scatter_ring(product_local(reflection, moving_all, 0, -1.0), "row", rows, 1)
        plus_field = own.astype(jnp.float32) + window(summed_up, onset_up)
        focus_low = plus_field.astype(jnp.bfloat16)
    return tuple(
        field.reshape(field.shape[0], 2, freqs, field.shape[2]) for field in (minus_field, plus_field)
    )


def solution(mesh):
    return jax.shard_map(
        functools.partial(body, mesh.shape["row"], mesh.shape["col"]),
        mesh=mesh,
        in_specs=(
            P(None, None, "row", "col"),
            P("row", None, None, "col"),
            P("col", "row"),
            P("row", "col"),
        ),
        out_specs=(P("col", None, None, "row"), P("row", None, None, "col")),
        check_vma=False,
    )
```
